32 devices in a mesh: dp: 8 (over z, x), mp: 4 (over y, core).
Axes of the slice: x: 2, y: 2, z: 4, core: 2. Of those that a mesh axis runs over, the one named last changes fastest.
Arguments:
- embed_table: float32 [16, 4096, 256], P('mp', 'dp'), may hold values from -5 to 5
- accum: float32 [16, 4096], P('mp', 'dp'), may hold values from 0.1 to 3
- stale_grad: bfloat16 [16, 4096, 256], P('mp', 'dp'), may hold values from -6 to 6
- grad_owner: int32 [16, 4096, 1], P('mp', 'dp'), may hold values from 0 to 7; in each aligned block of 512 rows (0 to 511, 512 to 1023, ..., all dimensions but the last counted through in order) at most 128 rows name the same one
- grad_row: int32 [16, 4096], P('mp', 'dp'), may hold values from 0 to 511
- lookup_owner: int32 [16, 4096, 1], P('mp', 'dp'), may hold values from 0 to 7; in each aligned block of 512 rows (0 to 511, 512 to 1023, ..., all dimensions but the last counted through in order) at most 128 rows name the same one
- lookup_row: int32 [16, 4096], P('mp', 'dp'), may hold values from 0 to 511
- bag_len: int32 [16, 2048], P('mp', 'dp'), may hold values from 1 to 2
- label: int32 [2048], P('dp'), may hold values 0 or 1
- up_factor_weight: bfloat16 [2, 512, 4096], P(None, None, 'mp'), may hold values from -0.25 to 0.25
- v_weight: bfloat16 [2, 512, 4096], P(None, None, 'mp'), may hold values from -0.09375 to 0.09375
- cross_bias: float32 [2, 4096], P(None, 'mp'), may hold values from -3 to 3
- head_weight: float32 [4096], P('mp'), may hold values from -0.09375 to 0.09375
Outputs:
- new_table: float32 [16, 4096, 256], P('mp', 'dp')
- new_accum: float32 [16, 4096], P('mp', 'dp')
- grad_u: float32 [2, 512, 4096], P(None, 'dp', 'mp')
- grad_v: float32 [2, 512, 4096], P(None, 'dp', 'mp')
- grad_small: float32 [3, 4096], P(None, 'mp')
- grad_pooled: bfloat16 [2048, 4096], P('dp', 'mp')
The draws below stay inside these ranges and needn't reach their ends.
Inputs may be any that keep to these rules, and one draw needn't show every extreme that they name: `grad_owner`: among the 512 blocks of one feature held by one index of dp, at most 128 name the same owner, and in some such group exactly 128 do. `lookup_owner`: among the 512 id slots of one feature belonging to one index of dp, at most 128 name the same owner, and in some such group exactly 128 do; slots k >= bag_len are unused.
All inputs are finite; a program needn't handle non-finite values. No bound on the sum of `label` on one device may be relied on, other than what follows from the above.
Results may differ from the reference program's by a relative error of at most 0.009.
Values may be sent and summed in bfloat16 or wider, within the bound.
A program may use at most 128 MiB of HBM per device.

```python
import math
import jax
import jax.numpy as jnp
import numpy as np
from jax import lax

E = 256
F = 16
R = 512
LC = 2
BAG = 2
B_DEV = 256
ROWS_DEV = 512
GR_DEV = 512
D0 = 4096
BATCH = 2048
ROWS = 4096
GR = 4096
LOOK = 4096
GCAP = 128
LCAP = 128
N_DP = 8


def plant(entries, key, least, high):
    dims = entries.shape
    spot = [jax.random.randint(jax.random.fold_in(key, axis), (), 0, dims[axis]) for axis in range(len(dims))]
    entries = entries.at[tuple(spot)].set(least)
    longest = dims.index(max(dims))
    spot[longest] = (spot[longest] + 1) % dims[longest]
    return entries.at[tuple(spot)].set(high)


def level_of(key, extent, split, least, top_value):
    gain, own = 1.0, jax.random.fold_in(key, 6)
    for dim, shards_of in split:
        draws = jnp.exp(jax.random.uniform(jax.random.fold_in(own, dim), (shards_of,), jnp.float32, least / len(split), top_value / len(split)))
        gain = gain * jnp.repeat(draws, extent[dim] // shards_of).reshape([-1 if axis == dim else 1 for axis in range(len(extent))])
    return gain


def rank_table(amount, lean):
    weights = [(1 << 20) // math.isqrt(grade ** lean) + 1 for grade in range(1, amount + 1)]
    deviation = 1 + sum(weights) // (1 << 30)
    return np.cumsum(np.array([max(1, weight // deviation) for weight in weights]))


def ranked(own_key, shape, count, lean):
    grid = rank_table(count, lean)
    pick = jax.random.randint(jax.random.fold_in(own_key, 1), shape, 0, int(grid[count - 1]))
    grade = jnp.searchsorted(jnp.asarray(grid, jnp.int32), pick, side="right")
    return jax.random.permutation(jax.random.fold_in(own_key, 2), count)[grade].astype(jnp.int32)


def deal_out(stream_key, own, number, rows, count, top, bound, skew):
    order = jax.random.permutation(stream_key, count)
    crowded, ordinary = shares(count, rows * top, bound, skew, True), shares(count, rows * top, bound, skew, False)
    places = jnp.arange(count)

    def named(tallies, rotation):
        used = int((tallies > 0).sum())
        fixed = max(1, used // 4)
        shifted = fixed + (places - fixed + rotation * (used - fixed)) % max(1, count - fixed)
        return jnp.zeros((count,), jnp.int32).at[order[jnp.where(places < fixed, places, shifted)]].set(jnp.asarray(tallies, jnp.int32))

    tallies = jnp.where(number % 4 == 0, named(crowded, number // 4), named(ordinary, number - number // 4 - 1))
    mixed = jax.random.permutation(jax.random.fold_in(own, 3), count)
    donor, taker = mixed[0:count // 2 * 2:2], mixed[1:count // 2 * 2:2]
    room = jnp.minimum(tallies[donor] - 1, bound - tallies[taker]) // 2
    room = jnp.where((donor == order[0]) | (taker == order[0]) | (tallies[taker] == 0), 0, jnp.maximum(room, 0))
    shifted = jax.random.randint(jax.random.fold_in(own, 4), (count // 2,), 0, 1 << 20) % (room + 1)
    tallies = tallies.at[donor].add(-shifted).at[taker].add(shifted)
    labels = jnp.searchsorted(jnp.cumsum(tallies), jnp.arange(rows * top), side="right").astype(jnp.int32)
    grid = labels.reshape(top, rows).T
    grid = grid[jax.random.permutation(jax.random.fold_in(own, 1), rows)]
    rotation = jax.random.randint(jax.random.fold_in(own, 2), (rows, 1), 0, top)
    return jnp.take_along_axis(grid, (jnp.arange(top)[None, :] + rotation) % top, axis=1)


def shares(amount, total, limit, skew, full):
    weights = [(1 << 20) // math.isqrt(grade ** skew) + 1 for grade in range(1, amount + 1)]
    largest = limit if full else min(limit, max(-(-total // amount), total * weights[0] // sum(weights)))
    least = 1 if total - largest >= amount - 1 else 0
    holding, surplus = [largest] + [least] * (amount - 1), total - largest - least * (amount - 1)
    while surplus > 0:
        movable = [i for i in range(1, amount) if holding[i] < largest] or [i for i in range(1, amount) if holding[i] < limit]
        pool, remaining = sum([weights[i] for i in movable]), surplus
        for i in movable:
            more = min(limit - holding[i], max(1, remaining * weights[i] // pool), surplus)
            holding[i] = holding[i] + more
            surplus = surplus - more
    return np.array(holding)


def noise(key, dims, width, most, shards=(), kind=jnp.bfloat16):
    result = jax.random.normal(key, dims, jnp.float32) * width
    if len(shards) > 0:
        result = level_of(key, dims, shards, -0.22, 0.18) * result
    return jnp.clip(result, min=-most, max=most).astype(kind)


def setup_inputs(seed: int = 0) -> dict:
    arg_keys = jax.random.split(jax.random.key(seed), 14)
    embed_table = noise(arg_keys[0], (F, ROWS, E), 0.7, 5.0, ((0, 4), (1, 8)), jnp.float32)
    accum = jnp.clip(jnp.exp(math.log(3.0) - 3.4011974 * jax.random.uniform(arg_keys[1], (F, ROWS), jnp.float32) ** level_of(arg_keys[1], (F, ROWS), ((0, 4), (1, 8)), -0.2, 0.2)), 0.1, 3.0)
    stale_grad = noise(arg_keys[2], (F, GR, E), 1.0, 6.0, ((0, 4), (1, 8)))
    grad_owner_keys = jax.random.split(jax.random.fold_in(arg_keys[3], 1), F * GR // GR_DEV)
    grad_owner_turns = jax.random.permutation(jax.random.fold_in(arg_keys[3], 3), F * GR // GR_DEV)
    grad_owner = jax.vmap(lambda own, number: deal_out(jax.random.fold_in(arg_keys[3], 2), own, number, GR_DEV, N_DP, 1, GCAP, 2))(grad_owner_keys, grad_owner_turns).reshape((F, GR, 1))
    grad_row = plant(ranked(arg_keys[4], (F, GR), ROWS_DEV, 2), jax.random.fold_in(arg_keys[4], 3), 0, ROWS_DEV - 1).astype(jnp.int32)
    lookup_owner_keys = jax.random.split(jax.random.fold_in(arg_keys[5], 1), F * LOOK // (B_DEV * BAG))
    lookup_owner_turns = jax.random.permutation(jax.random.fold_in(arg_keys[5], 3), F * LOOK // (B_DEV * BAG))
    lookup_owner = jax.vmap(lambda own, number: deal_out(jax.random.fold_in(arg_keys[5], 2), own, number, B_DEV * BAG, N_DP, 1, LCAP, 1))(lookup_owner_keys, lookup_owner_turns).reshape((F, LOOK, 1))
    lookup_row = plant(ranked(arg_keys[6], (F, LOOK), ROWS_DEV, 2), jax.random.fold_in(arg_keys[6], 3), 0, ROWS_DEV - 1).astype(jnp.int32)
    bag_len = plant(jax.random.randint(arg_keys[7], (F, BATCH), 1, BAG + 1), jax.random.fold_in(arg_keys[7], 1), 1, BAG).astype(jnp.int32)
    label = plant((jax.random.randint(arg_keys[8], (BATCH,), 0, 4) < 1).astype(jnp.int32), jax.random.fold_in(arg_keys[8], 1), 0, 1)
    up_factor_weight = noise(arg_keys[9], (LC, R, D0), R ** -0.5, 0.25, ((2, 4),))
    v_weight = noise(arg_keys[10], (LC, R, D0), D0 ** -0.5, 0.09375, ((2, 4),))
    cross_bias = noise(arg_keys[11], (LC, D0), 0.5, 3.0, ((1, 4),), jnp.float32)
    head_weight = noise(arg_keys[12], (D0,), D0 ** -0.5, 0.09375, ((0, 4),), jnp.float32)
    return dict(embed_table=embed_table, accum=accum, stale_grad=stale_grad, grad_owner=grad_owner, grad_row=grad_row, lookup_owner=lookup_owner, lookup_row=lookup_row, bag_len=bag_len, label=label, up_factor_weight=up_factor_weight, v_weight=v_weight, cross_bias=cross_bias, head_weight=head_weight)


learn_rate = 0.5

def adagrad_per_feature(packed):
    table_part, accum_part, grads, target = packed
    summed = jnp.zeros((ROWS, E), jnp.float32).at[target].add(grads.astype(jnp.float32))
    fresh_accum = accum_part + lax.optimization_barrier(jnp.mean(summed * summed, axis=1))
    fresh_table = table_part - learn_rate * summed / jnp.sqrt(fresh_accum)[:, None]
    return (fresh_table, fresh_accum)

def pool_feature(packed):
    table_part, target, counts = packed
    fetched = table_part[target].astype(jnp.bfloat16)
    fetched = lax.optimization_barrier(fetched).astype(jnp.float32).reshape(BATCH, BAG, E)
    inside = (jnp.arange(BAG)[None, :] < counts[:, None]).astype(jnp.float32)
    return lax.optimization_barrier(jnp.sum(fetched * inside[:, :, None], axis=1)).astype(jnp.bfloat16)

def reference(embed_table, accum, stale_grad, grad_owner, grad_row, lookup_owner, lookup_row, bag_len, label, up_factor_weight, v_weight, cross_bias, head_weight):
    grad_target = (grad_owner[:, :, 0] * ROWS_DEV + grad_row).astype(jnp.int32)
    new_table, new_accum = lax.map(adagrad_per_feature, (embed_table, accum, stale_grad, grad_target))
    look_target = (lookup_owner[:, :, 0] * ROWS_DEV + lookup_row).astype(jnp.int32)
    pooled = lax.map(pool_feature, (embed_table, look_target, bag_len))
    start = jnp.transpose(pooled, (1, 0, 2)).reshape(BATCH, D0)
    start_f = start.astype(jnp.float32)
    state = start
    states = []
    downs = []
    crosses = []
    for layer in range(LC):
        down_sum = jnp.dot(state, v_weight[layer].T, preferred_element_type=jnp.float32).astype(jnp.bfloat16)
        cross_out = jnp.dot(down_sum, up_factor_weight[layer], preferred_element_type=jnp.float32) + cross_bias[layer]
        states.append(state)
        downs.append(down_sum)
        crosses.append(cross_out)
        state = (start_f * cross_out + state.astype(jnp.float32)).astype(jnp.bfloat16)
    logit = lax.optimization_barrier(jnp.sum(state.astype(jnp.float32) * head_weight[None, :], axis=1))
    slope = (jax.nn.sigmoid(logit) - label.astype(jnp.float32)) / jnp.sqrt(jnp.float32(BATCH))
    upstream = slope[:, None] * head_weight[None, :]
    head_grad = lax.optimization_barrier(jnp.sum(slope[:, None] * state.astype(jnp.float32), axis=0))
    to_start = jnp.zeros((BATCH, D0), jnp.float32)
    grads_u = [None] * LC
    grads_v = [None] * LC
    bias_grads = [None] * LC
    for layer in reversed(range(LC)):
        direct = upstream * start_f
        bias_grads[layer] = lax.optimization_barrier(jnp.sum(direct, axis=0))
        direct_bias_term = direct.astype(jnp.bfloat16)
        grads_u[layer] = jnp.dot(downs[layer].T, direct_bias_term, preferred_element_type=jnp.float32)
        back_sum = jnp.dot(direct_bias_term, up_factor_weight[layer].T, preferred_element_type=jnp.float32).astype(jnp.bfloat16)
        grads_v[layer] = jnp.dot(back_sum.T, states[layer], preferred_element_type=jnp.float32)
        to_start = to_start + upstream * crosses[layer]
        upstream = upstream + jnp.dot(back_sum, v_weight[layer], preferred_element_type=jnp.float32)
    grad_pooled = (upstream + to_start).astype(jnp.bfloat16)
    grad_small = jnp.stack(bias_grads + [head_grad])
    return (new_table, new_accum, jnp.stack(grads_u), jnp.stack(grads_v), grad_small, grad_pooled)
```

```python
import functools

import jax
import jax.numpy as jnp
from jax import lax
from jax.experimental import pallas as pl
from jax.experimental.pallas import tpu as pltpu
from jax.sharding import PartitionSpec as P

learn_rate = 0.5


def bucket_slots(owners, capacity, peers):
    count = owners.shape[1]
    onehot = (owners[:, None, :] == jnp.arange(peers)[None, :, None]).astype(jnp.bfloat16)
    earlier = (jnp.arange(count)[:, None] < jnp.arange(count)[None, :]).astype(jnp.bfloat16)
    before = jnp.einsum("fpi,ij->fpj", onehot, earlier, preferred_element_type=jnp.float32)
    order_in = jnp.sum(before * onehot.astype(jnp.float32), axis=1)
    return owners * capacity + order_in.astype(jnp.int32)


def selection_matrix(indices, length):
    return (indices[:, :, None] == jnp.arange(length)[None, None, :]).astype(jnp.bfloat16)


def contract_last(left, right):
    return lax.dot_general(
        left, right, (((1,), (1,)), ((), ())), preferred_element_type=jnp.float32
    )


def contract_first(left, right):
    return lax.dot_general(
        left, right, (((0,), (0,)), ((), ())), preferred_element_type=jnp.float32
    )


def cross_down(state, v_layer):
    return lax.psum(contract_last(state, v_layer), "mp").astype(jnp.bfloat16)


def local(
    embed_table,
    accum,
    stale_grad,
    grad_owner,
    grad_row,
    lookup_owner,
    lookup_row,
    bag_len,
    label,
    up_factor_weight,
    v_weight,
    cross_bias,
    head_weight,
):
    peers = lax.axis_size("dp")
    local_feats, grad_dev, width = stale_grad.shape
    rows_per_shard = embed_table.shape[1]
    which_feature = jnp.arange(local_feats)[:, None]
    grad_cap = max(2, 2 * grad_dev // peers)
    grad_total = peers * grad_cap
    grad_slot = bucket_slots(grad_owner[:, :, 0], grad_cap, peers)
    place = selection_matrix(grad_slot, grad_total)
    send_grads = jnp.einsum(
        "fns,fne->fse", place, stale_grad, preferred_element_type=jnp.float32
    ).astype(jnp.bfloat16)
    send_rows = (
        jnp.full((local_feats, grad_total), rows_per_shard, jnp.int32)
        .at[which_feature, grad_slot]
        .set(grad_row)
    )
    recv_grads = lax.all_to_all(
        send_grads.reshape(local_feats, peers, grad_cap, width),
        "dp",
        split_axis=1,
        concat_axis=1,
        tiled=True,
    )
    recv_rows = lax.all_to_all(
        send_rows.reshape(local_feats, peers, grad_cap),
        "dp",
        split_axis=1,
        concat_axis=1,
        tiled=True,
    )
    landing = selection_matrix(recv_rows.reshape(local_feats, grad_total), rows_per_shard)
    summed = jnp.einsum(
        "wjc,wjl->wcl",
        landing,
        recv_grads.reshape(local_feats, grad_total, width),
        preferred_element_type=jnp.float32,
    )
    new_accum = accum + jnp.mean(summed * summed, axis=2)
    new_table = embed_table - learn_rate * summed / jnp.sqrt(new_accum)[:, :, None]
    batch_dev = bag_len.shape[1]
    look_dev = lookup_row.shape[1]
    bag_size = look_dev // batch_dev
    look_cap = max(2, 2 * look_dev // peers)
    look_total = peers * look_cap
    look_slot = bucket_slots(lookup_owner[:, :, 0], look_cap, peers)
    wanted = (
        jnp.zeros((local_feats, look_total), jnp.int32).at[which_feature, look_slot].set(lookup_row)
    )
    requested_ids = lax.all_to_all(
        wanted.reshape(local_feats, peers, look_cap), "dp", split_axis=1, concat_axis=1, tiled=True
    ).reshape(local_feats, look_total)
    second_table = embed_table.astype(jnp.bfloat16)
    served = jnp.einsum(
        "adv,avm->adm",
        selection_matrix(requested_ids, rows_per_shard),
        second_table,
        preferred_element_type=jnp.float32,
    ).astype(jnp.bfloat16)
    returned = lax.all_to_all(
        served.reshape(local_feats, peers, look_cap, width),
        "dp",
        split_axis=1,
        concat_axis=1,
        tiled=True,
    ).reshape(local_feats, look_total, width)
    slots = look_slot.reshape(local_feats, batch_dev, bag_size)
    mixing = jnp.zeros((local_feats, batch_dev, look_total), jnp.bfloat16)
    for member in range(bag_size):
        used = (bag_len > member).astype(jnp.bfloat16)
        mixing = mixing + selection_matrix(slots[:, :, member], look_total) * used[:, :, None]
    pooled = jnp.einsum(
        "fbs,fse->fbe", mixing, returned, preferred_element_type=jnp.float32
    ).astype(jnp.bfloat16)
    start = jnp.transpose(pooled, (1, 0, 2)).reshape(batch_dev, local_feats * width)
    start_f = start.astype(jnp.float32)
    n_layers = up_factor_weight.shape[0]
    state = start
    states = []
    downs = []
    crosses = []
    for layer in range(n_layers):
        down_sum = cross_down(state, v_weight[layer])
        cross_out = (
            jnp.dot(down_sum, up_factor_weight[layer], preferred_element_type=jnp.float32)
            + cross_bias[layer]
        )
        states.append(state)
        downs.append(down_sum)
        crosses.append(cross_out)
        state = (start_f * cross_out + state.astype(jnp.float32)).astype(jnp.bfloat16)
    logit = lax.psum(jnp.sum(state.astype(jnp.float32) * head_weight[None, :], axis=1), "mp")
    slope = (jax.nn.sigmoid(logit) - label.astype(jnp.float32)) / jnp.sqrt(
        jnp.float32(batch_dev * peers)
    )
    upstream = slope[:, None] * head_weight[None, :]
    head_grad = jnp.sum(slope[:, None] * state.astype(jnp.float32), axis=0)
    to_start = jnp.zeros(start_f.shape, jnp.float32)
    grads_u = [None] * n_layers
    grads_v = [None] * n_layers
    bias_grads = [None] * n_layers
    for layer in reversed(range(n_layers)):
        direct = upstream * start_f
        bias_grads[layer] = jnp.sum(direct, axis=0)
        direct_bias_term = direct.astype(jnp.bfloat16)
        grad_u_layer = contract_first(downs[layer], direct_bias_term)
        back_sum = lax.psum(contract_last(direct_bias_term, up_factor_weight[layer]), "mp").astype(
            jnp.bfloat16
        )
        down_factor_gradient = contract_first(back_sum, states[layer])
        to_start = to_start + upstream * crosses[layer]
        upstream = upstream + jnp.dot(back_sum, v_weight[layer], preferred_element_type=jnp.float32)
        grads_u[layer] = grad_u_layer
        grads_v[layer] = down_factor_gradient
    grad_u = jnp.stack(grads_u)
    grad_v = jnp.stack(grads_v)
    grad_u, grad_v = (
        lax.psum_scatter(grad_u, "dp", scatter_dimension=1, tiled=True),
        lax.psum_scatter(grad_v, "dp", scatter_dimension=1, tiled=True),
    )
    grad_small = lax.psum(jnp.stack(bias_grads + [head_grad]), "dp")
    grad_pooled = (upstream + to_start).astype(jnp.bfloat16)
    return (new_table, new_accum, grad_u, grad_v, grad_small, grad_pooled)


F32, BF16 = jnp.float32, jnp.bfloat16
MESH = pl.DeviceIdType.MESH


def one_hot_rows(count, first, row):
    spots = lax.broadcasted_iota(jnp.int32, (count, row.shape[1]), 0) + first
    return jnp.where(spots == row, 1.0, 0.0).astype(BF16)


def fused_kernel(
    batch_total,
    table_ref,
    accum_ref,
    stale_ref,
    gown_ref,
    grow_ref,
    lown_ref,
    lrow_ref,
    len_ref,
    label_ref,
    u_ref,
    v_ref,
    bias_ref,
    head_ref,
    new_table_ref,
    new_accum_ref,
    gu_ref,
    gv_ref,
    small_ref,
    pooled_ref,
    meta_tx,
    meta_rx,
    srv_tx,
    srv_rx,
    g_tx,
    g_rx,
    pool_acc,
    start,
    st1,
    st2,
    cr,
    up2,
    up1,
    db,
    dn,
    bk,
    tx1,
    rx1,
    tx2,
    rx2,
    ltx,
    lrx,
    slope_s,
    small_tx,
    small_rx,
    x_tx,
    x_rx,
    own,
    z_tx,
    z_rx,
    meta_ss,
    meta_rs,
    srv_ss,
    srv_rs,
    g_ss,
    g_rs,
    ar_ss,
    ar_rs,
    l_ss,
    l_rs,
    small_ss,
    small_rs,
    x_ss,
    x_rs,
    z_ss,
    z_rs,
):
    d = lax.axis_index("dp")
    m = lax.axis_index("mp")
    peers = meta_tx.shape[0]
    feats, rows, width = table_ref.shape
    count = gown_ref.shape[1]
    cap = meta_tx.shape[2]
    batch, cols = start.shape
    half = batch // 2
    chunk = 256
    x = lax.rem(d, 2)
    z = d // 2
    core = lax.rem(m, 2)
    nz = peers // 2

    def dp_peer(i):
        return {"dp": lax.rem(d + i, peers)}

    def z_peer(i):
        return {"dp": lax.rem(z + i, nz) * 2 + x}

    def remote(src, dst, ss, rs, dev):
        return pltpu.make_async_remote_copy(
            src_ref=src, dst_ref=dst, send_sem=ss, recv_sem=rs, device_id=dev, device_id_type=MESH
        )

    barrier = pltpu.get_barrier_semaphore()
    for i in range(1, peers):
        pl.semaphore_signal(barrier, inc=1, device_id=dp_peer(i), device_id_type=MESH)
    for i in range(1, 4):
        pl.semaphore_signal(
            barrier, inc=1, device_id={"mp": lax.rem(m + i, 4)}, device_id_type=MESH
        )

    peer_col = lax.broadcasted_iota(jnp.int32, (peers, count), 0)
    earlier = jnp.where(
        lax.broadcasted_iota(jnp.int32, (count, count), 0)
        < lax.broadcasted_iota(jnp.int32, (count, count), 1),
        1.0,
        0.0,
    ).astype(BF16)

    def order_of(owner):
        hot = jnp.where(peer_col == owner, 1.0, 0.0)
        before = jnp.dot(hot.astype(BF16), earlier, preferred_element_type=F32)
        return jnp.sum(before * hot, axis=0, keepdims=True)

    g_slots, l_slots, l_orders = [], [], []
    for f in range(feats):
        go, lo = gown_ref[f : f + 1, :], lown_ref[f : f + 1, :]
        g_slots.append(go * cap + order_of(go).astype(jnp.int32))
        l_orders.append(order_of(lo))
        l_slots.append(lo * cap + l_orders[-1].astype(jnp.int32))

    def split_row(row):
        hi = row // 256
        return [hi.astype(F32), (row - hi * 256).astype(F32)]

    pad = jnp.zeros((6, count), F32)

    def make_meta(p, _):
        for f in range(feats):
            for spot, slots, ref in ((f, l_slots[f], lrow_ref), (feats + f, g_slots[f], grow_ref)):
                hot = one_hot_rows(cap, p * cap, slots)
                vals = jnp.concatenate(split_row(ref[f : f + 1, :]) + [pad], axis=0).astype(BF16)
                res = lax.dot_general(
                    vals, hot, (((1,), (1,)), ((), ())), preferred_element_type=F32
                )
                meta_tx[p, spot : spot + 1, :] = (res[0:1] * 256.0 + res[1:2]).astype(jnp.int32)
        return 0

    lax.fori_loop(0, peers, make_meta, 0)
    pl.semaphore_wait(barrier, peers - 1 + 3)

    def meta_copy(i):
        return remote(
            meta_tx.at[lax.rem(d + i, peers)], meta_rx.at[i], meta_ss.at[i], meta_rs.at[i], dp_peer(i)
        )

    def srv_copy(i):
        return remote(srv_tx.at[i], srv_rx.at[i], srv_ss.at[i], srv_rs.at[i], dp_peer(peers - i))

    def g_copy(i):
        return remote(g_tx.at[i], g_rx.at[i], g_ss.at[i], g_rs.at[i], dp_peer(i))

    def loop_peers(body):
        def step(i, _):
            body(i)
            return 0

        lax.fori_loop(1, peers, step, 0)

    loop_peers(lambda i: meta_copy(i).start())
    meta_rx[0] = meta_tx[d]

    def pack(i, dst):
        p = lax.rem(d + i, peers)
        for f in range(feats):
            dst[i, f] = jnp.dot(
                one_hot_rows(cap, p * cap, g_slots[f]), stale_ref[f], preferred_element_type=F32
            ).astype(BF16)

    pack(0, g_rx)
    loop_peers(lambda i: pack(i, g_tx))

    def serve(i, dst):
        for f in range(feats):
            hot = one_hot_rows(rows, 0, meta_rx[i, f : f + 1, :])
            dst[i, f] = lax.dot_general(
                hot,
                table_ref[f].astype(BF16),
                (((0,), (0,)), ((), ())),
                preferred_element_type=F32,
            ).astype(BF16)

    def serve_peer(i):
        meta_copy(i).wait_recv()
        serve(i, srv_tx)
        srv_copy(i).start()

    loop_peers(serve_peer)
    serve(0, srv_rx)

    packed = jnp.concatenate(
        [lown_ref[f : f + 1, :].astype(F32) for f in range(feats)] + l_orders, axis=0
    ).astype(BF16)
    bag = count // batch
    pick_n = lax.broadcasted_iota(jnp.int32, (count, batch), 0)
    pick_b = lax.broadcasted_iota(jnp.int32, (count, batch), 1)
    member_slots = []
    for k in range(bag):
        pick = jnp.where(pick_n == pick_b * bag + k, 1.0, 0.0).astype(BF16)
        got = jnp.dot(packed, pick, preferred_element_type=F32)
        slot = (got[:feats] * float(cap) + got[feats:]).astype(jnp.int32)
        member_slots.append(jnp.where(len_ref[...] > k, slot, -1))

    def pool(i):
        p = lax.rem(d + i, peers)
        spots = lax.broadcasted_iota(jnp.int32, (cap, batch), 0) + p * cap
        for f in range(feats):
            mix = jnp.zeros((cap, batch), F32)
            for k in range(bag):
                mix = mix + jnp.where(spots == member_slots[k][f : f + 1, :], 1.0, 0.0)
            part = lax.dot_general(
                mix.astype(BF16),
                srv_rx[i, f],
                (((0,), (0,)), ((), ())),
                preferred_element_type=F32,
            )
            pool_acc[:, f * width : (f + 1) * width] += part

    pool_acc[...] = jnp.zeros_like(pool_acc)
    pool(0)

    def pool_peer(i):
        srv_copy(i).wait_recv()
        pool(i)

    loop_peers(pool_peer)
    loop_peers(lambda i: g_copy(i).start())
    start[...] = pool_acc[...].astype(BF16)

    mine = pl.ds(pl.multiple_of(core * half, half), half)
    other = pl.ds(pl.multiple_of((1 - core) * half, half), half)
    core_peer = {"mp": m + 1 - 2 * core}
    y_peer = {"mp": lax.rem(m + 2, 4)}

    def reduce_mp(r, left, right, dst, beside):
        nt = (((1,), (1,)), ((), ()))
        tx1[r] = lax.dot_general(left[other, :], right, nt, preferred_element_type=F32).astype(BF16)
        one = remote(tx1.at[r], rx1.at[r], ar_ss.at[r, 0], ar_rs.at[r, 0], core_peer)
        one.start()
        part = lax.dot_general(left[mine, :], right, nt, preferred_element_type=F32)
        one.wait_recv()
        tx2[r] = (part + rx1[r].astype(F32)).astype(BF16)
        two = remote(tx2.at[r], rx2.at[r], ar_ss.at[r, 1], ar_rs.at[r, 1], y_peer)
        two.start()
        beside()
        two.wait_recv()
        dst[mine, :] = (tx2[r].astype(F32) + rx2[r].astype(F32)).astype(BF16)
        three = remote(dst.at[mine, :], dst.at[mine, :], ar_ss.at[r, 2], ar_rs.at[r, 2], core_peer)
        three.start()
        three.wait_recv()
        one.wait_send()
        two.wait_send()
        three.wait_send()

    def loop_chunks(body):
        def step(j, _):
            body(pl.ds(pl.multiple_of(j * chunk, chunk), chunk))
            return 0

        lax.fori_loop(0, cols // chunk, step, 0)

    states = [start, st1, st2]
    slope_s[...] = jnp.zeros_like(slope_s)
    for layer in range(2):
        reduce_mp(layer, states[layer], v_ref[layer], dn.at[layer], lambda: None)

        def forward(at, layer=layer):
            cross = (
                jnp.dot(dn[layer], u_ref[layer, :, at], preferred_element_type=F32)
                + bias_ref[layer : layer + 1, at]
            )
            cr[layer, :, at] = cross
            nxt = start[:, at].astype(F32) * cross + states[layer][:, at].astype(F32)
            states[layer + 1][:, at] = nxt.astype(BF16)
            if layer == 1:
                term = nxt.astype(BF16).astype(F32) * head_ref[:, at]
                slope_s[...] += term[:, 0:128] + term[:, 128:256]

        loop_chunks(forward)

    column = jnp.sum(slope_s[...], axis=1, keepdims=True)
    wide = jnp.transpose(jnp.broadcast_to(column, (batch, 128)))
    ltx[...] = wide[0:8, :]
    logit_copies = [
        remote(ltx, lrx.at[i], l_ss.at[i], l_rs.at[i], {"mp": lax.rem(m + i, 4)})
        for i in range(1, 4)
    ]
    for copy in logit_copies:
        copy.start()
    for copy in logit_copies:
        copy.wait_recv()
    logit = ltx[0:1, :] + lrx[1, 0:1, :] + lrx[2, 0:1, :] + lrx[3, 0:1, :]
    slope_row = (jax.nn.sigmoid(logit) - label_ref[...].astype(F32)) / jnp.sqrt(F32(batch_total))
    slope_s[...] = jnp.transpose(jnp.broadcast_to(slope_row, (128, batch)))

    block = gu_ref.shape[1]

    def x_copy(q):
        return remote(x_tx.at[q], x_rx.at[q], x_ss.at[q], x_rs.at[q], {"dp": d + 1 - 2 * x})

    def z_copy(q, i):
        return remote(
            z_tx.at[q, lax.rem(z + i, nz)],
            z_rx.at[q, i - 1],
            z_ss.at[q, i - 1],
            z_rs.at[q, i - 1],
            z_peer(i),
        )

    def factor(q, left, right):
        def step(j, _):
            at = pl.ds(pl.multiple_of(j * 2 * block, 2 * block), 2 * block)
            res = lax.dot_general(
                left[:, at], right[...], (((0,), (0,)), ((), ())), preferred_element_type=F32
            )
            lower, upper = res[:block], res[block:]
            own[q, j] = jnp.where(x == 0, lower, upper)
            x_tx[q, j] = jnp.where(x == 0, upper, lower).astype(BF16)
            return 0

        lax.fori_loop(0, nz, step, 0)
        x_copy(q).start()

    def merge(q):
        x_copy(q).wait_recv()

        def step(j, _):
            total = own[q, j] + x_rx[q, j].astype(F32)
            own[q, j] = total
            z_tx[q, j] = total.astype(BF16)
            return 0

        lax.fori_loop(0, nz, step, 0)
        for i in range(1, nz):
            z_copy(q, i).start()

    def finish(q, out, layer):
        for i in range(1, nz):
            z_copy(q, i).wait_recv()
        total = own[q, z]
        for i in range(1, nz):
            total = total + z_rx[q, i - 1].astype(F32)
        out[layer] = total

    small_tx[...] = jnp.zeros_like(small_tx)

    def top(at):
        slope = slope_s[:, 0:1]
        up = slope * head_ref[:, at]
        direct = up * start[:, at].astype(F32)
        up2[:, at] = up
        db[1, :, at] = direct.astype(BF16)
        small_tx[1:2, at] = jnp.sum(direct, axis=0, keepdims=True)
        small_tx[2:3, at] = jnp.sum(slope * st2[:, at].astype(F32), axis=0, keepdims=True)

    loop_chunks(top)
    reduce_mp(2, db.at[1], u_ref[1], bk.at[1], lambda: factor(0, dn.at[1], db.at[1]))

    def middle(at):
        up = up2[:, at] + jnp.dot(bk[1], v_ref[1, :, at], preferred_element_type=F32)
        direct = up * start[:, at].astype(F32)
        up1[:, at] = up
        db[0, :, at] = direct.astype(BF16)
        small_tx[0:1, at] = jnp.sum(direct, axis=0, keepdims=True)

    loop_chunks(middle)

    def small_copy(i):
        return remote(small_tx, small_rx.at[i], small_ss.at[i], small_rs.at[i], dp_peer(i))

    def beside_last():
        factor(1, bk.at[1], st1)
        factor(2, dn.at[0], db.at[0])
        merge(0)

    reduce_mp(3, db.at[0], u_ref[0], bk.at[0], beside_last)
    factor(3, bk.at[0], start)
    loop_peers(lambda i: small_copy(i).start())
    merge(1)

    def bottom(at):
        up = up1[:, at] + jnp.dot(bk[0], v_ref[0, :, at], preferred_element_type=F32)
        pooled_ref[:, at] = (
            up + (up2[:, at] * cr[1, :, at] + up1[:, at] * cr[0, :, at])
        ).astype(BF16)

    loop_chunks(bottom)
    merge(2)
    merge(3)

    loop_peers(lambda i: g_copy(i).wait_recv())

    def update(f, _):
        def add(i, total):
            hot = one_hot_rows(rows, 0, meta_rx[i, pl.ds(feats + f, 1), :])
            return total + jnp.dot(hot, g_rx[i, f], preferred_element_type=F32)

        summed = lax.fori_loop(0, peers, add, jnp.zeros((rows, width), F32))
        mean = jnp.sum(summed * summed, axis=1, keepdims=True) * (1.0 / width)
        before = jnp.transpose(jnp.broadcast_to(accum_ref[pl.ds(f, 1), :], (128, rows)))[:, 0:1]
        fresh = before + mean
        new_accum_ref[pl.ds(f, 1), :] = jnp.transpose(jnp.broadcast_to(fresh, (rows, 128)))[0:1, :]
        new_table_ref[f] = table_ref[f] - summed * (learn_rate / jnp.sqrt(fresh))
        return 0

    lax.fori_loop(0, feats, update, 0)

    loop_peers(lambda i: small_copy(i).wait_recv())
    total = small_tx[...]
    for i in range(1, peers):
        total = total + small_rx[i]
    small_ref[...] = total
    finish(0, gu_ref, 1)
    finish(1, gv_ref, 1)
    finish(2, gu_ref, 0)
    finish(3, gv_ref, 0)

    def drain(i):
        meta_copy(i).wait_send()
        srv_copy(i).wait_send()
        g_copy(i).wait_send()
        small_copy(i).wait_send()

    loop_peers(drain)
    for copy in logit_copies:
        copy.wait_send()
    for q in range(4):
        x_copy(q).wait_send()
        for i in range(1, nz):
            z_copy(q, i).wait_send()


def fused_local(
    embed_table,
    accum,
    stale_grad,
    grad_owner,
    grad_row,
    lookup_owner,
    lookup_row,
    bag_len,
    label,
    up_factor_weight,
    v_weight,
    cross_bias,
    head_weight,
):
    peers = lax.axis_size("dp")
    feats, rows, width = embed_table.shape
    count = stale_grad.shape[1]
    cap = 2 * count // peers
    batch = bag_len.shape[1]
    layers, rank, cols = v_weight.shape
    block = rank // peers
    half = batch // 2
    nz = peers // 2
    dma = pltpu.SemaphoreType.DMA
    vmem = pl.BlockSpec(memory_space=pltpu.VMEM)
    shape = jax.ShapeDtypeStruct
    outs = pl.pallas_call(
        functools.partial(fused_kernel, batch * peers),
        out_shape=[
            shape((feats, rows, width), F32),
            shape((feats, rows), F32),
            shape((layers, block, cols), F32),
            shape((layers, block, cols), F32),
            shape((8, cols), F32),
            shape((batch, cols), BF16),
        ],
        in_specs=[vmem] * 13,
        out_specs=[vmem] * 6,
        scratch_shapes=[
            pltpu.VMEM((peers, 2 * feats, cap), jnp.int32),
            pltpu.VMEM((peers, 2 * feats, cap), jnp.int32),
            pltpu.VMEM((peers, feats, cap, width), BF16),
            pltpu.VMEM((peers, feats, cap, width), BF16),
            pltpu.VMEM((peers, feats, cap, width), BF16),
            pltpu.VMEM((peers, feats, cap, width), BF16),
            pltpu.VMEM((batch, cols), F32),
            pltpu.VMEM((batch, cols), BF16),
            pltpu.VMEM((batch, cols), BF16),
            pltpu.VMEM((batch, cols), BF16),
            pltpu.VMEM((2, batch, cols), F32),
            pltpu.VMEM((batch, cols), F32),
            pltpu.VMEM((batch, cols), F32),
            pltpu.VMEM((2, batch, cols), BF16),
            pltpu.VMEM((2, batch, rank), BF16),
            pltpu.VMEM((2, batch, rank), BF16),
            pltpu.VMEM((4, half, rank), BF16),
            pltpu.VMEM((4, half, rank), BF16),
            pltpu.VMEM((4, half, rank), BF16),
            pltpu.VMEM((4, half, rank), BF16),
            pltpu.VMEM((8, batch), F32),
            pltpu.VMEM((4, 8, batch), F32),
            pltpu.VMEM((batch, 128), F32),
            pltpu.VMEM((8, cols), F32),
            pltpu.VMEM((peers, 8, cols), F32),
            pltpu.VMEM((4, nz, block, cols), BF16),
            pltpu.VMEM((4, nz, block, cols), BF16),
            pltpu.VMEM((4, nz, block, cols), F32),
            pltpu.VMEM((4, nz, block, cols), BF16),
            pltpu.VMEM((4, nz - 1, block, cols), BF16),
            dma((peers,)),
            dma((peers,)),
            dma((peers,)),
            dma((peers,)),
            dma((peers,)),
            dma((peers,)),
            dma((4, 3)),
            dma((4, 3)),
            dma((4,)),
            dma((4,)),
            dma((peers,)),
            dma((peers,)),
            dma((4,)),
            dma((4,)),
            dma((4, nz - 1)),
            dma((4, nz - 1)),
        ],
        compiler_params=pltpu.CompilerParams(
            collective_id=0, has_side_effects=True, vmem_limit_bytes=60 * 1024 * 1024
        ),
    )(
        embed_table,
        accum,
        stale_grad,
        grad_owner[:, :, 0],
        grad_row,
        lookup_owner[:, :, 0],
        lookup_row,
        bag_len,
        label.reshape(1, batch),
        up_factor_weight,
        v_weight,
        cross_bias,
        head_weight.reshape(1, cols),
    )
    new_table, new_accum, grad_u, grad_v, grad_small, grad_pooled = outs
    return new_table, new_accum, grad_u, grad_v, grad_small[:3], grad_pooled


def solution(mesh):
    fits = mesh.shape["dp"] == 8 and mesh.shape["mp"] == 4
    return jax.shard_map(
        fused_local if fits else local,
        mesh=mesh,
        in_specs=(
            P("mp", "dp", None),
            P("mp", "dp"),
            P("mp", "dp", None),
            P("mp", "dp", None),
            P("mp", "dp"),
            P("mp", "dp", None),
            P("mp", "dp"),
            P("mp", "dp"),
            P("dp"),
            P(None, None, "mp"),
            P(None, None, "mp"),
            P(None, "mp"),
            P("mp"),
        ),
        out_specs=(
            P("mp", "dp", None),
            P("mp", "dp"),
            P(None, "dp", "mp"),
            P(None, "dp", "mp"),
            P(None, "mp"),
            P("dp", "mp"),
        ),
        check_vma=False,
    )
```

```python
import functools

import jax
import jax.numpy as jnp
from jax import lax
from jax.experimental import pallas as pl
from jax.experimental.pallas import tpu as pltpu
from jax.sharding import PartitionSpec as P

learn_rate = 0.5


def bucket_slots(owners, capacity, peers):
    count = owners.shape[1]
    onehot = (owners[:, None, :] == jnp.arange(peers)[None, :, None]).astype(jnp.bfloat16)
    earlier = (jnp.arange(count)[:, None] < jnp.arange(count)[None, :]).astype(jnp.bfloat16)
    before = jnp.einsum("fpi,ij->fpj", onehot, earlier, preferred_element_type=jnp.float32)
    order_in = jnp.sum(before * onehot.astype(jnp.float32), axis=1)
    return owners * capacity + order_in.astype(jnp.int32)


def selection_matrix(indices, length):
    return (indices[:, :, None] == jnp.arange(length)[None, None, :]).astype(jnp.bfloat16)


def contract_last(left, right):
    return lax.dot_general(
        left, right, (((1,), (1,)), ((), ())), preferred_element_type=jnp.float32
    )


def contract_first(left, right):
    return lax.dot_general(
        left, right, (((0,), (0,)), ((), ())), preferred_element_type=jnp.float32
    )


def cross_down(state, v_layer):
    return lax.psum(contract_last(state, v_layer), "mp").astype(jnp.bfloat16)


def local(
    embed_table,
    accum,
    stale_grad,
    grad_owner,
    grad_row,
    lookup_owner,
    lookup_row,
    bag_len,
    label,
    up_factor_weight,
    v_weight,
    cross_bias,
    head_weight,
):
    peers = lax.axis_size("dp")
    local_feats, grad_dev, width = stale_grad.shape
    rows_per_shard = embed_table.shape[1]
    which_feature = jnp.arange(local_feats)[:, None]
    grad_cap = max(2, 2 * grad_dev // peers)
    grad_total = peers * grad_cap
    grad_slot = bucket_slots(grad_owner[:, :, 0], grad_cap, peers)
    place = selection_matrix(grad_slot, grad_total)
    send_grads = jnp.einsum(
        "fns,fne->fse", place, stale_grad, preferred_element_type=jnp.float32
    ).astype(jnp.bfloat16)
    send_rows = (
        jnp.full((local_feats, grad_total), rows_per_shard, jnp.int32)
        .at[which_feature, grad_slot]
        .set(grad_row)
    )
    recv_grads = lax.all_to_all(
        send_grads.reshape(local_feats, peers, grad_cap, width),
        "dp",
        split_axis=1,
        concat_axis=1,
        tiled=True,
    )
    recv_rows = lax.all_to_all(
        send_rows.reshape(local_feats, peers, grad_cap),
        "dp",
        split_axis=1,
        concat_axis=1,
        tiled=True,
    )
    landing = selection_matrix(recv_rows.reshape(local_feats, grad_total), rows_per_shard)
    summed = jnp.einsum(
        "wjc,wjl->wcl",
        landing,
        recv_grads.reshape(local_feats, grad_total, width),
        preferred_element_type=jnp.float32,
    )
    new_accum = accum + jnp.mean(summed * summed, axis=2)
    new_table = embed_table - learn_rate * summed / jnp.sqrt(new_accum)[:, :, None]
    batch_dev = bag_len.shape[1]
    look_dev = lookup_row.shape[1]
    bag_size = look_dev // batch_dev
    look_cap = max(2, 2 * look_dev // peers)
    look_total = peers * look_cap
    look_slot = bucket_slots(lookup_owner[:, :, 0], look_cap, peers)
    wanted = (
        jnp.zeros((local_feats, look_total), jnp.int32).at[which_feature, look_slot].set(lookup_row)
    )
    requested_ids = lax.all_to_all(
        wanted.reshape(local_feats, peers, look_cap), "dp", split_axis=1, concat_axis=1, tiled=True
    ).reshape(local_feats, look_total)
    second_table = embed_table.astype(jnp.bfloat16)
    served = jnp.einsum(
        "adv,avm->adm",
        selection_matrix(requested_ids, rows_per_shard),
        second_table,
        preferred_element_type=jnp.float32,
    ).astype(jnp.bfloat16)
    returned = lax.all_to_all(
        served.reshape(local_feats, peers, look_cap, width),
        "dp",
        split_axis=1,
        concat_axis=1,
        tiled=True,
    ).reshape(local_feats, look_total, width)
    slots = look_slot.reshape(local_feats, batch_dev, bag_size)
    mixing = jnp.zeros((local_feats, batch_dev, look_total), jnp.bfloat16)
    for member in range(bag_size):
        used = (bag_len > member).astype(jnp.bfloat16)
        mixing = mixing + selection_matrix(slots[:, :, member], look_total) * used[:, :, None]
    pooled = jnp.einsum(
        "fbs,fse->fbe", mixing, returned, preferred_element_type=jnp.float32
    ).astype(jnp.bfloat16)
    start = jnp.transpose(pooled, (1, 0, 2)).reshape(batch_dev, local_feats * width)
    start_f = start.astype(jnp.float32)
    n_layers = up_factor_weight.shape[0]
    state = start
    states = []
    downs = []
    crosses = []
    for layer in range(n_layers):
        down_sum = cross_down(state, v_weight[layer])
        cross_out = (
            jnp.dot(down_sum, up_factor_weight[layer], preferred_element_type=jnp.float32)
            + cross_bias[layer]
        )
        states.append(state)
        downs.append(down_sum)
        crosses.append(cross_out)
        state = (start_f * cross_out + state.astype(jnp.float32)).astype(jnp.bfloat16)
    logit = lax.psum(jnp.sum(state.astype(jnp.float32) * head_weight[None, :], axis=1), "mp")
    slope = (jax.nn.sigmoid(logit) - label.astype(jnp.float32)) / jnp.sqrt(
        jnp.float32(batch_dev * peers)
    )
    upstream = slope[:, None] * head_weight[None, :]
    head_grad = jnp.sum(slope[:, None] * state.astype(jnp.float32), axis=0)
    to_start = jnp.zeros(start_f.shape, jnp.float32)
    grads_u = [None] * n_layers
    grads_v = [None] * n_layers
    bias_grads = [None] * n_layers
    for layer in reversed(range(n_layers)):
        direct = upstream * start_f
        bias_grads[layer] = jnp.sum(direct, axis=0)
        direct_bias_term = direct.astype(jnp.bfloat16)
        grad_u_layer = contract_first(downs[layer], direct_bias_term)
        back_sum = lax.psum(contract_last(direct_bias_term, up_factor_weight[layer]), "mp").astype(
            jnp.bfloat16
        )
        down_factor_gradient = contract_first(back_sum, states[layer])
        to_start = to_start + upstream * crosses[layer]
        upstream = upstream + jnp.dot(back_sum, v_weight[layer], preferred_element_type=jnp.float32)
        grads_u[layer] = grad_u_layer
        grads_v[layer] = down_factor_gradient
    grad_u = jnp.stack(grads_u)
    grad_v = jnp.stack(grads_v)
    grad_u, grad_v = (
        lax.psum_scatter(grad_u, "dp", scatter_dimension=1, tiled=True),
        lax.psum_scatter(grad_v, "dp", scatter_dimension=1, tiled=True),
    )
    grad_small = lax.psum(jnp.stack(bias_grads + [head_grad]), "dp")
    grad_pooled = (upstream + to_start).astype(jnp.bfloat16)
    return (new_table, new_accum, grad_u, grad_v, grad_small, grad_pooled)


F32, BF16 = jnp.float32, jnp.bfloat16
MESH = pl.DeviceIdType.MESH


def one_hot_rows(count, first, row):
    spots = lax.broadcasted_iota(jnp.int32, (count, row.shape[1]), 0) + first
    return jnp.where(spots == row, 1.0, 0.0).astype(BF16)


def fused_kernel(
    batch_total,
    table_ref,
    accum_ref,
    stale_ref,
    gown_ref,
    grow_ref,
    lown_ref,
    lrow_ref,
    len_ref,
    label_ref,
    u_ref,
    v_ref,
    bias_ref,
    head_ref,
    new_table_ref,
    new_accum_ref,
    gu_ref,
    gv_ref,
    small_ref,
    pooled_ref,
    meta_tx,
    meta_rx,
    gmeta_tx,
    gmeta_rx,
    table_s,
    srv_tx,
    srv_rx,
    g_tx,
    g_rx,
    pool_acc,
    start,
    st1,
    st2,
    cr,
    up2,
    up1,
    db,
    dn,
    bk,
    tx1,
    rx1,
    tx2,
    rx2,
    ltx,
    lrx,
    slope_s,
    small_tx,
    small_rx,
    x_tx,
    x_rx,
    own,
    z_tx,
    z_rx,
    meta_ss,
    meta_rs,
    gmeta_ss,
    gmeta_rs,
    srv_ss,
    srv_rs,
    g_ss,
    g_rs,
    ar_ss,
    ar_rs,
    l_ss,
    l_rs,
    small_ss,
    small_rs,
    x_ss,
    x_rs,
    z_ss,
    z_rs,
):
    d = lax.axis_index("dp")
    m = lax.axis_index("mp")
    peers = meta_tx.shape[0]
    feats, rows, width = table_ref.shape
    count = gown_ref.shape[1]
    cap = meta_tx.shape[2]
    batch, cols = start.shape
    half = batch // 2
    chunk = 256
    x = lax.rem(d, 2)
    z = d // 2
    core = lax.rem(m, 2)
    nz = peers // 2

    def dp_peer(i):
        return {"dp": lax.rem(d + i, peers)}

    def z_peer(i):
        return {"dp": lax.rem(z + i, nz) * 2 + x}

    def remote(src, dst, ss, rs, dev):
        return pltpu.make_async_remote_copy(
            src_ref=src, dst_ref=dst, send_sem=ss, recv_sem=rs, device_id=dev, device_id_type=MESH
        )

    barrier = pltpu.get_barrier_semaphore()
    for i in range(1, peers):
        pl.semaphore_signal(barrier, inc=1, device_id=dp_peer(i), device_id_type=MESH)
    for i in range(1, 4):
        pl.semaphore_signal(
            barrier, inc=1, device_id={"mp": lax.rem(m + i, 4)}, device_id_type=MESH
        )

    peer_col = lax.broadcasted_iota(jnp.int32, (peers, count), 0)
    earlier = jnp.where(
        lax.broadcasted_iota(jnp.int32, (count, count), 0)
        < lax.broadcasted_iota(jnp.int32, (count, count), 1),
        1.0,
        0.0,
    ).astype(BF16)

    def order_of(owner):
        hot = jnp.where(peer_col == owner, 1.0, 0.0)
        before = jnp.dot(hot.astype(BF16), earlier, preferred_element_type=F32)
        return jnp.sum(before * hot, axis=0, keepdims=True)

    g_slots, l_slots, l_orders = [], [], []
    for f in range(feats):
        lo = lown_ref[f : f + 1, :]
        l_orders.append(order_of(lo))
        l_slots.append(lo * cap + l_orders[-1].astype(jnp.int32))

    def split_row(row):
        hi = row // 256
        return [hi.astype(F32), (row - hi * 256).astype(F32)]

    pad = jnp.zeros((6, count), F32)

    def rows_in_slots(ref, f, hot):
        vals = jnp.concatenate(split_row(ref[f : f + 1, :]) + [pad], axis=0).astype(BF16)
        res = lax.dot_general(vals, hot, (((1,), (1,)), ((), ())), preferred_element_type=F32)
        return (res[0:1] * 256.0 + res[1:2]).astype(jnp.int32)

    def g_copy(i):
        return remote(g_tx.at[i], g_rx.at[i], g_ss.at[i], g_rs.at[i], dp_peer(i))

    def send_grads(first, last):
        for i in range(first, last):
            gmeta_copy(i).start()
            g_copy(i).start()

    def ask(i, dst):
        p = lax.rem(d + i, peers)
        for f in range(feats):
            hot = one_hot_rows(cap, p * cap, l_slots[f])
            dst[i, f : f + 1, :] = rows_in_slots(lrow_ref, f, hot)

    def meta_copy(i):
        return remote(meta_tx.at[i], meta_rx.at[i], meta_ss.at[i], meta_rs.at[i], dp_peer(i))

    def gmeta_copy(i):
        return remote(gmeta_tx.at[i], gmeta_rx.at[i], gmeta_ss.at[i], gmeta_rs.at[i], dp_peer(i))

    def srv_copy(i):
        return remote(srv_tx.at[i], srv_rx.at[i], srv_ss.at[i], srv_rs.at[i], dp_peer(peers - i))

    def loop_peers(body):
        def step(i, _):
            body(i)
            return 0

        lax.fori_loop(1, peers, step, 0)

    pl.semaphore_wait(barrier, peers - 1 + 3)

    def ask_peer(i):
        ask(i, meta_tx)
        meta_copy(i).start()

    loop_peers(ask_peer)
    ask(0, meta_rx)
    for f in range(feats):
        table_s[f] = table_ref[f].astype(BF16)

    def serve(i, dst):
        for f in range(feats):
            hot = one_hot_rows(rows, 0, meta_rx[i, f : f + 1, :])
            dst[i, f] = lax.dot_general(
                hot,
                table_s[f],
                (((0,), (0,)), ((), ())),
                preferred_element_type=F32,
            ).astype(BF16)

    def serve_peer(i):
        meta_copy(i).wait_recv()
        serve(i, srv_tx)
        srv_copy(i).start()

    for f in range(feats):
        owner = gown_ref[f : f + 1, :]
        g_slots.append(owner * cap + order_of(owner).astype(jnp.int32))

    def pack(i, dst, ids):
        p = lax.rem(d + i, peers)
        for f in range(feats):
            hot = one_hot_rows(cap, p * cap, g_slots[f])
            dst[i, f] = jnp.dot(hot, stale_ref[f], preferred_element_type=F32).astype(BF16)
            ids[i, f : f + 1, :] = rows_in_slots(grow_ref, f, hot)

    for i in range(1, 3):
        pack(i, g_tx, gmeta_tx)
        send_grads(i, i + 1)

    loop_peers(serve_peer)

    pack(0, g_rx, gmeta_rx)
    def pack_peer(i, _):
        pack(i, g_tx, gmeta_tx)
        return 0

    lax.fori_loop(3, peers, pack_peer, 0)
    serve(0, srv_rx)

    packed = jnp.concatenate(
        [lown_ref[f : f + 1, :].astype(F32) for f in range(feats)] + l_orders, axis=0
    ).astype(BF16)
    bag = count // batch
    pick_n = lax.broadcasted_iota(jnp.int32, (count, batch), 0)
    pick_b = lax.broadcasted_iota(jnp.int32, (count, batch), 1)
    member_slots = []
    for k in range(bag):
        pick = jnp.where(pick_n == pick_b * bag + k, 1.0, 0.0).astype(BF16)
        got = jnp.dot(packed, pick, preferred_element_type=F32)
        slot = (got[:feats] * float(cap) + got[feats:]).astype(jnp.int32)
        member_slots.append(jnp.where(len_ref[...] > k, slot, -1))

    def pool(i):
        p = lax.rem(d + i, peers)
        spots = lax.broadcasted_iota(jnp.int32, (cap, batch), 0) + p * cap
        for f in range(feats):
            mix = jnp.zeros((cap, batch), F32)
            for k in range(bag):
                mix = mix + jnp.where(spots == member_slots[k][f : f + 1, :], 1.0, 0.0)
            part = lax.dot_general(
                mix.astype(BF16),
                srv_rx[i, f],
                (((0,), (0,)), ((), ())),
                preferred_element_type=F32,
            )
            pool_acc[:, f * width : (f + 1) * width] += part

    pool_acc[...] = jnp.zeros_like(pool_acc)
    pool(0)

    def pool_peer(i):
        srv_copy(i).wait_recv()
        pool(i)

    loop_peers(pool_peer)
    send_grads(3, peers)
    start[...] = pool_acc[...].astype(BF16)

    mine = pl.ds(pl.multiple_of(core * half, half), half)
    other = pl.ds(pl.multiple_of((1 - core) * half, half), half)
    core_peer = {"mp": m + 1 - 2 * core}
    y_peer = {"mp": lax.rem(m + 2, 4)}

    def reduce_mp(r, left, right, dst, beside):
        nt = (((1,), (1,)), ((), ()))
        tx1[r] = lax.dot_general(left[other, :], right, nt, preferred_element_type=F32).astype(BF16)
        one = remote(tx1.at[r], rx1.at[r], ar_ss.at[r, 0], ar_rs.at[r, 0], core_peer)
        one.start()
        part = lax.dot_general(left[mine, :], right, nt, preferred_element_type=F32)
        one.wait_recv()
        tx2[r] = (part + rx1[r].astype(F32)).astype(BF16)
        two = remote(tx2.at[r], rx2.at[r], ar_ss.at[r, 1], ar_rs.at[r, 1], y_peer)
        two.start()
        beside()
        two.wait_recv()
        dst[mine, :] = (tx2[r].astype(F32) + rx2[r].astype(F32)).astype(BF16)
        three = remote(dst.at[mine, :], dst.at[mine, :], ar_ss.at[r, 2], ar_rs.at[r, 2], core_peer)
        three.start()
        three.wait_recv()
        one.wait_send()
        two.wait_send()
        three.wait_send()

    def loop_chunks(body):
        def step(j, _):
            body(pl.ds(pl.multiple_of(j * chunk, chunk), chunk))
            return 0

        lax.fori_loop(0, cols // chunk, step, 0)

    states = [start, st1, st2]
    slope_s[...] = jnp.zeros_like(slope_s)
    for layer in range(2):
        reduce_mp(layer, states[layer], v_ref[layer], dn.at[layer], lambda: None)

        def forward(at, layer=layer):
            cross = (
                jnp.dot(dn[layer], u_ref[layer, :, at], preferred_element_type=F32)
                + bias_ref[layer : layer + 1, at]
            )
            cr[layer, :, at] = cross
            nxt = start[:, at].astype(F32) * cross + states[layer][:, at].astype(F32)
            states[layer + 1][:, at] = nxt.astype(BF16)
            if layer == 1:
                term = nxt.astype(BF16).astype(F32) * head_ref[:, at]
                slope_s[...] += term[:, 0:128] + term[:, 128:256]

        loop_chunks(forward)

    column = jnp.sum(slope_s[...], axis=1, keepdims=True)
    wide = jnp.transpose(jnp.broadcast_to(column, (batch, 128)))
    ltx[...] = wide[0:8, :]
    logit_copies = [
        remote(ltx, lrx.at[i], l_ss.at[i], l_rs.at[i], {"mp": lax.rem(m + i, 4)})
        for i in range(1, 4)
    ]
    for copy in logit_copies:
        copy.start()
    for copy in logit_copies:
        copy.wait_recv()
    logit = ltx[0:1, :] + lrx[1, 0:1, :] + lrx[2, 0:1, :] + lrx[3, 0:1, :]
    slope_row = (jax.nn.sigmoid(logit) - label_ref[...].astype(F32)) / jnp.sqrt(F32(batch_total))
    slope_s[...] = jnp.transpose(jnp.broadcast_to(slope_row, (128, batch)))

    block = gu_ref.shape[1]

    def x_copy(q):
        return remote(x_tx.at[q], x_rx.at[q], x_ss.at[q], x_rs.at[q], {"dp": d + 1 - 2 * x})

    def z_copy(q, i):
        return remote(
            z_tx.at[q, lax.rem(z + i, nz)],
            z_rx.at[q, i - 1],
            z_ss.at[q, i - 1],
            z_rs.at[q, i - 1],
            z_peer(i),
        )

    def factor(q, left, right):
        def step(j, _):
            at = pl.ds(pl.multiple_of(j * 2 * block, 2 * block), 2 * block)
            res = lax.dot_general(
                left[:, at], right[...], (((0,), (0,)), ((), ())), preferred_element_type=F32
            )
            lower, upper = res[:block], res[block:]
            own[q, j] = jnp.where(x == 0, lower, upper)
            x_tx[q, j] = jnp.where(x == 0, upper, lower).astype(BF16)
            return 0

        lax.fori_loop(0, nz, step, 0)
        x_copy(q).start()

    def merge(q):
        x_copy(q).wait_recv()

        def step(j, _):
            total = own[q, j] + x_rx[q, j].astype(F32)
            own[q, j] = total
            z_tx[q, j] = total.astype(BF16)
            return 0

        lax.fori_loop(0, nz, step, 0)
        for i in range(1, nz):
            z_copy(q, i).start()

    def finish(q, out, layer):
        for i in range(1, nz):
            z_copy(q, i).wait_recv()
        total = own[q, z]
        for i in range(1, nz):
            total = total + z_rx[q, i - 1].astype(F32)
        out[layer] = total

    small_tx[...] = jnp.zeros_like(small_tx)

    def top(at):
        slope = slope_s[:, 0:1]
        up = slope * head_ref[:, at]
        direct = up * start[:, at].astype(F32)
        up2[:, at] = up
        db[1, :, at] = direct.astype(BF16)
        small_tx[1:2, at] = jnp.sum(direct, axis=0, keepdims=True)
        small_tx[2:3, at] = jnp.sum(slope * st2[:, at].astype(F32), axis=0, keepdims=True)

    loop_chunks(top)
    reduce_mp(2, db.at[1], u_ref[1], bk.at[1], lambda: factor(0, dn.at[1], db.at[1]))

    def middle(at):
        up = up2[:, at] + jnp.dot(bk[1], v_ref[1, :, at], preferred_element_type=F32)
        direct = up * start[:, at].astype(F32)
        up1[:, at] = up
        db[0, :, at] = direct.astype(BF16)
        small_tx[0:1, at] = jnp.sum(direct, axis=0, keepdims=True)

    loop_chunks(middle)

    def small_copy(i):
        return remote(small_tx, small_rx.at[i], small_ss.at[i], small_rs.at[i], dp_peer(i))

    def beside_last():
        factor(1, bk.at[1], st1)
        factor(2, dn.at[0], db.at[0])
        merge(0)

    reduce_mp(3, db.at[0], u_ref[0], bk.at[0], beside_last)
    factor(3, bk.at[0], start)
    loop_peers(lambda i: small_copy(i).start())
    merge(1)

    def bottom(at):
        up = up1[:, at] + jnp.dot(bk[0], v_ref[0, :, at], preferred_element_type=F32)
        pooled_ref[:, at] = (
            up + (up2[:, at] * cr[1, :, at] + up1[:, at] * cr[0, :, at])
        ).astype(BF16)

    loop_chunks(bottom)
    merge(2)
    merge(3)

    def landed(i):
        gmeta_copy(i).wait_recv()
        g_copy(i).wait_recv()

    loop_peers(landed)

    def update(f, _):
        def add(i, total):
            hot = one_hot_rows(rows, 0, gmeta_rx[i, pl.ds(f, 1), :])
            return total + jnp.dot(hot, g_rx[i, f], preferred_element_type=F32)

        summed = lax.fori_loop(0, peers, add, jnp.zeros((rows, width), F32))
        mean = jnp.sum(summed * summed, axis=1, keepdims=True) * (1.0 / width)
        before = jnp.transpose(jnp.broadcast_to(accum_ref[pl.ds(f, 1), :], (128, rows)))[:, 0:1]
        fresh = before + mean
        new_accum_ref[pl.ds(f, 1), :] = jnp.transpose(jnp.broadcast_to(fresh, (rows, 128)))[0:1, :]
        new_table_ref[f] = table_ref[f] - summed * (learn_rate / jnp.sqrt(fresh))
        return 0

    lax.fori_loop(0, feats, update, 0)

    loop_peers(lambda i: small_copy(i).wait_recv())
    total = small_tx[...]
    for i in range(1, peers):
        total = total + small_rx[i]
    small_ref[...] = total
    finish(0, gu_ref, 1)
    finish(1, gv_ref, 1)
    finish(2, gu_ref, 0)
    finish(3, gv_ref, 0)

    def drain(i):
        meta_copy(i).wait_send()
        gmeta_copy(i).wait_send()
        srv_copy(i).wait_send()
        g_copy(i).wait_send()
        small_copy(i).wait_send()

    loop_peers(drain)
    for copy in logit_copies:
        copy.wait_send()
    for q in range(4):
        x_copy(q).wait_send()
        for i in range(1, nz):
            z_copy(q, i).wait_send()


def fused_local(
    embed_table,
    accum,
    stale_grad,
    grad_owner,
    grad_row,
    lookup_owner,
    lookup_row,
    bag_len,
    label,
    up_factor_weight,
    v_weight,
    cross_bias,
    head_weight,
):
    peers = lax.axis_size("dp")
    feats, rows, width = embed_table.shape
    count = stale_grad.shape[1]
    cap = 2 * count // peers
    batch = bag_len.shape[1]
    layers, rank, cols = v_weight.shape
    block = rank // peers
    half = batch // 2
    nz = peers // 2
    dma = pltpu.SemaphoreType.DMA
    vmem = pl.BlockSpec(memory_space=pltpu.VMEM)
    shape = jax.ShapeDtypeStruct
    outs = pl.pallas_call(
        functools.partial(fused_kernel, batch * peers),
        out_shape=[
            shape((feats, rows, width), F32),
            shape((feats, rows), F32),
            shape((layers, block, cols), F32),
            shape((layers, block, cols), F32),
            shape((8, cols), F32),
            shape((batch, cols), BF16),
        ],
        in_specs=[vmem] * 13,
        out_specs=[vmem] * 6,
        scratch_shapes=[
            pltpu.VMEM((peers, feats, cap), jnp.int32),
            pltpu.VMEM((peers, feats, cap), jnp.int32),
            pltpu.VMEM((peers, feats, cap), jnp.int32),
            pltpu.VMEM((peers, feats, cap), jnp.int32),
            pltpu.VMEM((feats, rows, width), BF16),
            pltpu.VMEM((peers, feats, cap, width), BF16),
            pltpu.VMEM((peers, feats, cap, width), BF16),
            pltpu.VMEM((peers, feats, cap, width), BF16),
            pltpu.VMEM((peers, feats, cap, width), BF16),
            pltpu.VMEM((batch, cols), F32),
            pltpu.VMEM((batch, cols), BF16),
            pltpu.VMEM((batch, cols), BF16),
            pltpu.VMEM((batch, cols), BF16),
            pltpu.VMEM((2, batch, cols), F32),
            pltpu.VMEM((batch, cols), F32),
            pltpu.VMEM((batch, cols), F32),
            pltpu.VMEM((2, batch, cols), BF16),
            pltpu.VMEM((2, batch, rank), BF16),
            pltpu.VMEM((2, batch, rank), BF16),
            pltpu.VMEM((4, half, rank), BF16),
            pltpu.VMEM((4, half, rank), BF16),
            pltpu.VMEM((4, half, rank), BF16),
            pltpu.VMEM((4, half, rank), BF16),
            pltpu.VMEM((8, batch), F32),
            pltpu.VMEM((4, 8, batch), F32),
            pltpu.VMEM((batch, 128), F32),
            pltpu.VMEM((8, cols), F32),
            pltpu.VMEM((peers, 8, cols), F32),
            pltpu.VMEM((4, nz, block, cols), BF16),
            pltpu.VMEM((4, nz, block, cols), BF16),
            pltpu.VMEM((4, nz, block, cols), F32),
            pltpu.VMEM((4, nz, block, cols), BF16),
            pltpu.VMEM((4, nz - 1, block, cols), BF16),
            dma((peers,)),
            dma((peers,)),
            dma((peers,)),
            dma((peers,)),
            dma((peers,)),
            dma((peers,)),
            dma((peers,)),
            dma((peers,)),
            dma((4, 3)),
            dma((4, 3)),
            dma((4,)),
            dma((4,)),
            dma((peers,)),
            dma((peers,)),
            dma((4,)),
            dma((4,)),
            dma((4, nz - 1)),
            dma((4, nz - 1)),
        ],
        compiler_params=pltpu.CompilerParams(
            collective_id=0, has_side_effects=True, vmem_limit_bytes=60 * 1024 * 1024
        ),
    )(
        embed_table,
        accum,
        stale_grad,
        grad_owner[:, :, 0],
        grad_row,
        lookup_owner[:, :, 0],
        lookup_row,
        bag_len,
        label.reshape(1, batch),
        up_factor_weight,
        v_weight,
        cross_bias,
        head_weight.reshape(1, cols),
    )
    new_table, new_accum, grad_u, grad_v, grad_small, grad_pooled = outs
    return new_table, new_accum, grad_u, grad_v, grad_small[:3], grad_pooled


def solution(mesh):
    fits = mesh.shape["dp"] == 8 and mesh.shape["mp"] == 4
    return jax.shard_map(
        fused_local if fits else local,
        mesh=mesh,
        in_specs=(
            P("mp", "dp", None),
            P("mp", "dp"),
            P("mp", "dp", None),
            P("mp", "dp", None),
            P("mp", "dp"),
            P("mp", "dp", None),
            P("mp", "dp"),
            P("mp", "dp"),
            P("dp"),
            P(None, None, "mp"),
            P(None, None, "mp"),
            P(None, "mp"),
            P("mp"),
        ),
        out_specs=(
            P("mp", "dp", None),
            P("mp", "dp"),
            P(None, "dp", "mp"),
            P(None, "dp", "mp"),
            P(None, "mp"),
            P("dp", "mp"),
        ),
        check_vma=False,
    )
```
